128 devices in a mesh: tile: 16 (over y, z), plane: 8 (over x, core).
Axes of the slice: x: 4, y: 4, z: 4, core: 2. Of those that a mesh axis runs over, the one named last changes fastest.
Arguments:
- reference_image: bfloat16 [512, 4096], P('plane', 'tile'), may hold values from -6 to 6
- source_images: bfloat16 [6, 512, 4096], P(None, 'plane', 'tile'), may hold values from -6 to 6
- warps: bfloat16 [6, 32, 4, 256, 4096], P(None, 'plane', None, None, 'tile'), may hold values from -0.1875 to 0.1875
- offsets: int32 [6, 32, 4, 16], P(None, 'plane', None, 'tile'), may hold values from -1 to 1
Outputs:
- cost_volume: float32 [32, 512, 4096], P('plane', None, 'tile')
- best_cost: float32 [512, 4096], P('plane', 'tile')
The draws below stay inside these ranges and needn't reach their ends.
All inputs are finite; a program needn't handle non-finite values.
Results may differ from the reference program's by a relative error of at most 0.0005.
Values may be sent and summed in bfloat16 or wider, within the bound.
A program may use at most 192 MiB of HBM per device.

```python
import jax
import jax.numpy as jnp
from jax import lax

TW = 256
ROWS = 512
VIEWS = 6
SLOTS = 4
HALF = 3
PLANES = 32
COLS = 4096
N_TILE = 16


def with_ends(drawn, own_key, least, top_value):
    extent = drawn.shape
    index_at = [jax.random.randint(jax.random.fold_in(own_key, axis), (), 0, extent[axis]) for axis in range(len(extent))]
    drawn = drawn.at[tuple(index_at)].set(least)
    longest = extent.index(max(extent))
    index_at[longest] = (index_at[longest] + 1) % extent[longest]
    return drawn.at[tuple(index_at)].set(top_value)


def block_scale(own_key, extent, shards, low, largest):
    def one(axis_at, shards_of):
        steps = jax.random.uniform(jax.random.fold_in(jax.random.fold_in(own_key, 6), axis_at), (shards_of,), jnp.float32, low / len(shards), largest / len(shards))
        return jnp.repeat(jnp.exp(steps), extent[axis_at] // shards_of).reshape((-1,) + (1,) * (len(extent) - axis_at - 1))

    factor_of = one(*shards[0])
    for cut in shards[1:]:
        factor_of = factor_of * one(*cut)
    return factor_of


def bell_draw(own_key, extent, deviation, bound, pieces=(), kind=jnp.bfloat16):
    entries = jax.random.normal(own_key, extent, jnp.float32) * deviation
    if len(pieces) > 0:
        entries = block_scale(own_key, extent, pieces, -0.22, 0.18) * entries
    return jnp.clip(entries, min=-bound, max=bound).astype(kind)


def setup_inputs(seed: int = 0) -> dict:
    streams_of = jax.random.split(jax.random.key(seed), 5)
    reference_image = bell_draw(streams_of[0], (ROWS, COLS), 1.0, 6.0, ((0, 8), (1, 16)))
    source_images = bell_draw(streams_of[1], (VIEWS, ROWS, COLS), 1.0, 6.0, ((1, 8), (2, 16)))
    warps = bell_draw(streams_of[2], (VIEWS, PLANES, SLOTS, TW, COLS), (TW * SLOTS) ** -0.5, 0.1875, ((1, 8), (4, 16)))
    offsets = with_ends(jax.random.randint(streams_of[3], (VIEWS, PLANES, SLOTS, N_TILE), -1, 2), jax.random.fold_in(streams_of[3], 1), -1, 1).astype(jnp.int32)
    return dict(reference_image=reference_image, source_images=source_images, warps=warps, offsets=offsets)


stabilizer = 4.0

def box_sum(values):
    height = values.shape[-2]
    width_all = values.shape[-1]
    leading = [(0, 0)] * (values.ndim - 2)
    padded = jnp.pad(values, leading + [(HALF, HALF), (0, 0)])
    rowed = padded[..., 0:height, :]
    for offset_row in range(1, 2 * HALF + 1):
        rowed = rowed + padded[..., offset_row:offset_row + height, :]
    padded = jnp.pad(rowed, leading + [(0, 0), (HALF, HALF)])
    summed = padded[..., 0:width_all]
    for offset_col in range(1, 2 * HALF + 1):
        summed = summed + padded[..., offset_col:offset_col + width_all]
    return summed

def correlation(sum_r, sum_rr, sum_w, sum_ww, sum_rw):
    count = float((2 * HALF + 1) ** 2)
    covar = sum_rw - sum_r * sum_w / count
    var_ref = sum_rr - sum_r * sum_r / count
    var_warp = sum_ww - sum_w * sum_w / count
    return covar * lax.rsqrt((var_ref + stabilizer) * (var_warp + stabilizer))

def reference(reference_image, source_images, warps, offsets):
    ref_float = reference_image.astype(jnp.float32)
    sum_r = box_sum(ref_float)
    sum_rr = box_sum(ref_float * ref_float)
    padded_src = jnp.pad(source_images, ((0, 0), (0, 0), (TW, TW)))
    tile_ids = jnp.arange(N_TILE, dtype=jnp.int32)

    def plane_cost(plane_id):
        matrices = lax.dynamic_index_in_dim(warps, plane_id, 1, keepdims=False)
        shifts = lax.dynamic_index_in_dim(offsets, plane_id, 1, keepdims=False)
        running = jnp.zeros((ROWS, TW * N_TILE), jnp.float32)
        for view_id in range(VIEWS):

            def tile_warp(tile_id):
                summed = jnp.zeros((ROWS, TW), jnp.float32)
                for slot_id in range(SLOTS):
                    first_col = ((tile_id + shifts[view_id, slot_id, tile_id] + 1) * TW).astype(jnp.int32)
                    source_block = lax.dynamic_slice_in_dim(padded_src[view_id], first_col, TW, 1)
                    matrix = lax.dynamic_slice_in_dim(matrices[view_id, slot_id], (tile_id * TW).astype(jnp.int32), TW, 1)
                    summed = summed + jnp.dot(source_block, matrix, preferred_element_type=jnp.float32)
                return summed
            tile_parts = lax.map(tile_warp, tile_ids)
            warped = jnp.transpose(tile_parts, (1, 0, 2)).reshape(ROWS, TW * N_TILE)
            normalized = correlation(sum_r, sum_rr, box_sum(warped), box_sum(warped * warped), box_sum(ref_float * warped))
            running = running + (1.0 - normalized)
        return running / VIEWS
    cost_volume = lax.map(plane_cost, jnp.arange(PLANES, dtype=jnp.int32))
    return (cost_volume, lax.optimization_barrier(jnp.min(cost_volume, axis=0)))
```

```python
import functools

import jax
import jax.numpy as jnp
from jax import lax
from jax.experimental import pallas as pl
from jax.experimental.pallas import tpu as pltpu
from jax.sharding import PartitionSpec as P

MESH = pl.DeviceIdType.MESH
HALF = 3
COUNT = float((2 * HALF + 1) ** 2)
STABILIZER = 4.0
TW = 256
SUB = 8
RUN = 32
PART = SUB * RUN
F32 = jnp.float32
BF16 = jnp.bfloat16


def iota(shape, dim):
    return lax.broadcasted_iota(jnp.int32, shape, dim)


def third(x):
    return (x * 171) >> 9


def as01(mask):
    return jnp.where(mask, 1.0, 0.0).astype(BF16)


def mm(a, b):
    return jnp.dot(a, b, preferred_element_type=F32)


def split2(x):
    hi = x.astype(BF16)
    return hi, (x - hi.astype(F32)).astype(BF16)


def body(
    views,
    planes,
    tiles,
    nq,
    ref_hbm,
    src_hbm,
    warp_hbm,
    off_ref,
    vol_hbm,
    best_ref,
    *scratch,
):
    srcs = scratch[:views]
    (
        ref_all,
        warp,
        picked,
        wb,
        rb,
        sums,
        acc,
        rn,
        inv,
        slab,
        slab16,
        halo,
        band,
        perm,
        unperm,
        edge_t,
        edge_q,
        esums,
        vol,
        low,
        got1,
        red,
        got2,
        s1_send,
        s1_recv,
        own_sem,
        z_send,
        z_recv,
        f_send,
        f_recv,
        w_sem,
        h_send,
        h_recv,
        m_send,
        m_recv,
        out_sem,
    ) = scratch[views:]
    nx = nq // 2
    rows = nq * ref_hbm.shape[0]
    halves = rows // PART
    t = lax.axis_index("tile")
    q = lax.axis_index("plane")
    x = q // 2
    c = q % 2
    sib = 2 * x + 1 - c
    has_left = t > 0
    has_right = t < tiles - 1
    left = lax.rem(t + tiles - 1, tiles)
    right = lax.rem(t + 1, tiles)

    def at_x(d):
        return lax.rem(x + d + nx, nx)

    def remote(src, dst, ssem, rsem, dev):
        return pltpu.make_async_remote_copy(
            src_ref=src,
            dst_ref=dst,
            send_sem=ssem,
            recv_sem=rsem,
            device_id=dev,
            device_id_type=MESH,
        )

    def piece(k):
        return ref_hbm if k == views else src_hbm.at[k]

    def slot(k, xx, cc):
        return ref_all.at[xx, cc] if k == views else srcs[k].at[1, xx, cc]

    def column(k, cc):
        if k == views:
            return ref_all.at[:, pl.ds(cc, 1)]
        return srcs[k].at[1, :, pl.ds(cc, 1)]

    def own_copy(k):
        return pltpu.make_async_copy(piece(k), slot(k, x, c), own_sem.at[k])

    def x_send(k, d):
        return remote(
            piece(k), slot(k, x, c), s1_send.at[k, d - 1], s1_recv.at[k, d - 1], (t, 2 * at_x(d) + c)
        )

    def x_arrival(k, d):
        return remote(
            piece(k), slot(k, at_x(-d), c), s1_send.at[k, d - 1], s1_recv.at[k, d - 1], (t, 2 * at_x(d) + c)
        )

    def z_copy(k, side):
        return remote(
            column(k, c),
            srcs[k].at[2 * side, :, pl.ds(c, 1)],
            z_send.at[k, side],
            z_recv.at[k, side],
            (right if side == 0 else left, q),
        )

    def to_sib(k, block):
        source = column(k, c) if block == 1 else srcs[k].at[block, :, pl.ds(c, 1)]
        return remote(source, source, f_send.at[k, block], f_recv.at[k, block], (t, sib))

    def from_sib(k, block):
        target = column(k, 1 - c) if block == 1 else srcs[k].at[block, :, pl.ds(1 - c, 1)]
        return remote(target, target, f_send.at[k, block], f_recv.at[k, block], (t, sib))

    def when_arrives(side, fn):
        pl.when(has_left if side == 0 else has_right)(fn)

    def when_sends(side, fn):
        pl.when(has_right if side == 0 else has_left)(fn)

    def stage1(k):
        for d in range(1, nx):
            x_send(k, d).start()
        own_copy(k).start()

    def stage2(k):
        own_copy(k).wait()
        for d in range(1, nx):
            x_arrival(k, d).wait_recv()
        if k < views:
            for side in (0, 1):
                when_sends(side, lambda side=side: z_copy(k, side).start())
        to_sib(k, 1).start()

    def stage3(k):
        for side in (0, 1):

            @functools.partial(when_arrives, side)
            def _():
                z_copy(k, side).wait_recv()
                to_sib(k, 2 * side).start()

    def finish(k):
        from_sib(k, 1).wait_recv()
        if k < views:
            for side in (0, 1):
                when_arrives(side, lambda side=side: from_sib(k, 2 * side).wait_recv())

    def drain(k):
        for d in range(1, nx):
            x_send(k, d).wait_send()
        to_sib(k, 1).wait_send()
        if k < views:
            for side in (0, 1):
                when_sends(side, lambda side=side: z_copy(k, side).wait_send())
                when_arrives(side, lambda side=side: to_sib(k, 2 * side).wait_send())

    def warp_copy(k):
        return pltpu.make_async_copy(warp_hbm.at[k], warp.at[k], w_sem.at[k])

    def halo_copy(side):
        return remote(
            slab16.at[side], halo.at[side], h_send.at[side], h_recv.at[side], (right if side == 0 else left, q)
        )

    barrier = pltpu.get_barrier_semaphore()
    partners = [(t, 2 * at_x(d) + c) for d in range(1, nx)] + [(t, sib), (left, q), (right, q)]
    for dev in partners:
        pl.semaphore_signal(barrier, inc=1, device_id=dev, device_id_type=MESH)
    pl.semaphore_wait(barrier, len(partners))

    stage1(0)
    stage1(views)
    warp_copy(0).start()
    for k in range(1, views):
        stage1(k)
    for k in range(1, views):
        warp_copy(k).start()

    ri, ci = iota((TW, TW), 0), iota((TW, TW), 1)
    band[...] = as01(jnp.abs(ri - ci) <= HALF)
    perm[...] = as01(((ri & (SUB - 1)) * RUN + (ri >> 3)) == ci)
    unperm[...] = as01(((ci & (SUB - 1)) * RUN + (ci >> 3)) == ri)
    rk, cl = iota((384, 128), 0), iota((384, 128), 1)
    kk = rk & 127
    ki, li = third(kk), third(cl)
    gap = (rk >> 7) * 3 - 3 + (kk - 3 * ki) - (cl - 3 * li)
    edge_t[...] = as01((ki == li) & (jnp.abs(gap) <= HALF))
    rq, cq = iota((128, 128), 0), iota((128, 128), 1)
    r_lane = 3 * views * planes
    edge_q[...] = as01(rq == r_lane + cq - 3 * third(cq))
    slab[...] = jnp.zeros_like(slab)
    acc[...] = jnp.zeros_like(acc)

    @pl.when(jnp.logical_not(has_left))
    def _():
        halo[0] = jnp.zeros_like(halo[0])
        for k in range(views):
            srcs[k][0] = jnp.zeros_like(srcs[k][0])

    @pl.when(jnp.logical_not(has_right))
    def _():
        halo[1] = jnp.zeros_like(halo[1])
        for k in range(views):
            srcs[k][2] = jnp.zeros_like(srcs[k][2])

    lane = iota((rows, 128), 1)

    def pack(w, i):
        first = 3 * i
        here = (lane >= first) & (lane < first + 3)
        wl, wr = w[:, :128], w[:, 128:]
        for n, (part, shift) in enumerate(((wl, 0), (wl, 125), (wr, 6), (wr, 3))):
            slab[n] = jnp.where(here, pltpu.roll(part, lax.rem(first + shift, 128), 1), slab[n])

    def permute(value):
        return jnp.concatenate(
            [mm(perm[...], value[PART * h : PART * (h + 1)]).astype(BF16) for h in range(halves)], axis=0
        )

    def put_sums(target, n, value):
        wide = value.shape[1]
        cells = value.reshape(halves, RUN, SUB, wide)
        sub = iota((HALF, SUB, wide), 1)
        target[n, :, HALF : HALF + RUN] = cells
        before = [pltpu.roll(cells[h, RUN - HALF :], 1, 1) for h in range(halves)]
        after = [pltpu.roll(cells[h, :HALF], SUB - 1, 1) for h in range(halves)]
        zero = jnp.zeros((HALF, SUB, wide), F32)
        for h in range(halves):
            target[n, h, :HALF] = jnp.where(sub == 0, before[h - 1] if h else zero, before[h])
            target[n, h, HALF + RUN :] = jnp.where(
                sub == SUB - 1, after[h + 1] if h + 1 < halves else zero, after[h]
            )

    def row_sums(source, n, h, first, size, lanes):
        v = source[n, h, pl.ds(first, size + 6), :, lanes]
        two = v[: size + 5] + v[1 : size + 6]
        four = two[:size] + two[2 : size + 2]
        return (four + two[4 : size + 4]) + v[6 : size + 6]

    stage2(0)
    stage2(views)
    if views > 1:
        stage2(1)
    finish(views)

    r = permute(ref_all[...].reshape(rows, TW))
    rb[...] = r
    rf = r.astype(F32)
    pack(rf, views * planes)
    rr_hi, rr_lo = split2(rf * rf)
    put_sums(sums, 0, mm(r, band[...]))
    put_sums(sums, 1, mm(rr_hi, band[...]) + mm(rr_lo, band[...]))
    every = pl.ds(0, TW)
    for h in range(halves):
        sr = row_sums(sums, 0, h, 0, RUN, every)
        srr = row_sums(sums, 1, h, 0, RUN, every)
        mean = sr * (1.0 / COUNT)
        rn[h] = mean
        inv[h] = lax.rsqrt(jnp.maximum(srr - sr * mean, 0.0) + STABILIZER)
    stage3(0)

    STEP = 16
    chunks = RUN // STEP

    def view_step(v, carry):
        for k in range(views):

            @pl.when(v == k)
            def _():
                if k + 2 < views:
                    stage2(k + 2)
                if k + 1 < views:
                    stage3(k + 1)
                finish(k)
                for b in range(3):
                    picked[b] = permute(srcs[k][b].reshape(rows, TW))
                warp_copy(k).wait()

        def resample(p, carry):
            w = None
            for s in range(4):
                block = off_ref[(v * planes + p) * 4 + s] + 1
                term = mm(picked[block], warp[v, p, s])
                w = term if w is None else w + term
            wb[p] = w.astype(BF16)
            pack(w, v * planes + p)
            return carry

        lax.fori_loop(0, planes, resample, 0)

        @pl.when(v == views - 1)
        def _():
            slab16[0] = slab[3].astype(BF16)
            slab16[1] = slab[0].astype(BF16)
            for side in (0, 1):
                when_sends(side, lambda side=side: halo_copy(side).start())

        def correlate(p, carry):
            w = wb[p]
            put_sums(sums, 0, mm(w, band[...]))
            put_sums(sums, 1, mm(w * w, band[...]))
            put_sums(sums, 2, mm(w * rb[...], band[...]))

            def part(n, carry):
                h = n // chunks
                first = (n % chunks) * STEP
                for lt in range(2):
                    lanes = pl.ds(128 * lt, 128)
                    sw = row_sums(sums, 0, h, first, STEP, lanes)
                    sww = row_sums(sums, 1, h, first, STEP, lanes)
                    srw = row_sums(sums, 2, h, first, STEP, lanes)
                    covar = srw - rn[h, pl.ds(first, STEP), :, lanes] * sw
                    var = jnp.maximum(sww - sw * (sw * (1.0 / COUNT)), 0.0) + STABILIZER
                    acc[p, h, pl.ds(first, STEP), :, lanes] += covar * lax.rsqrt(var)
                return carry

            lax.fori_loop(0, halves * chunks, part, 0)
            return carry

        lax.fori_loop(0, planes, correlate, 0)
        return carry

    lax.fori_loop(0, views, view_step, 0)

    for side in (0, 1):
        when_arrives(side, lambda side=side: halo_copy(side).wait_recv())

    edges = []
    for side in (0, 1):
        if side == 0:
            cells = [halo[0], slab[0].astype(BF16), slab[1].astype(BF16)]
        else:
            cells = [slab[2].astype(BF16), slab[3].astype(BF16), halo[1]]
        refs = [mm(cell, edge_q[...]).astype(BF16) for cell in cells]
        w, rw = jnp.concatenate(cells, axis=1), jnp.concatenate(refs, axis=1)
        wf, rf = w.astype(F32), rw.astype(F32)

        def summed(value):
            hi, lo = split2(value)
            return mm(hi, edge_t[...]) + mm(lo, edge_t[...])

        put_sums(esums, 0, mm(w, edge_t[...]))
        put_sums(esums, 1, summed(wf * wf))
        put_sums(esums, 2, summed(rf * wf))
        put_sums(esums, 3, mm(rw, edge_t[...]))
        put_sums(esums, 4, summed(rf * rf))
        out = []
        for h in range(halves):
            sw, sww, srw, sr, srr = [row_sums(esums, n, h, 0, RUN, pl.ds(0, 128)) for n in range(5)]
            covar = srw - sr * (sw * (1.0 / COUNT))
            var = jnp.maximum(sww - sw * (sw * (1.0 / COUNT)), 0.0) + STABILIZER
            var_r = jnp.maximum(srr - sr * (sr * (1.0 / COUNT)), 0.0) + STABILIZER
            ncc = covar * (lax.rsqrt(var) * lax.rsqrt(var_r))
            total = ncc
            for v in range(1, views):
                total = total + pltpu.roll(ncc, 128 - 3 * planes * v, 2)
            out.append(total)
        edges.append(out)

    lane3 = iota((RUN, SUB, 128), 2)

    def vol_copy(p):
        return pltpu.make_async_copy(vol.at[p], vol_hbm.at[p], out_sem.at[p])

    for p in range(planes):
        for h in range(halves):
            total = acc[p, h] * inv[h]
            lo_part, hi_part = total[:, :, :128], total[:, :, 128:]
            l_edge = pltpu.roll(edges[0][h], (128 - 3 * p) % 128, 2)
            r_edge = pltpu.roll(edges[1][h], 125 - 3 * p, 2)
            total = jnp.concatenate(
                [jnp.where(lane3 < 3, l_edge, lo_part), jnp.where(lane3 >= 125, r_edge, hi_part)], axis=2
            )
            hi, lo = split2((total * (1.0 / views)).reshape(PART, TW))
            cost = 1.0 - (mm(unperm[...], hi) + mm(unperm[...], lo))
            vol[p, PART * h : PART * (h + 1)] = cost
            per = PART * nx // rows
            cost4 = cost.reshape(per, 2, rows // nq, TW)
            spot = slice(per * h, per * (h + 1))
            low[spot] = cost4 if p == 0 else jnp.minimum(low[spot], cost4)
        vol_copy(p).start()

    swap = remote(low.at[:, pl.ds(1 - c, 1)], got1, m_send.at[0], m_recv.at[0], (t, sib))
    swap.start()
    swap.wait_recv()
    red[...] = jnp.minimum(low[:, pl.ds(c, 1)], got1[...])

    def min_copy(d):
        return remote(
            red.at[at_x(d)], got2.at[d - 1], m_send.at[d], m_recv.at[d], (t, 2 * at_x(d) + c)
        )

    for d in range(1, nx):
        min_copy(d).start()
    best = red[x, 0]
    for d in range(1, nx):
        min_copy(d).wait_recv()
        best = jnp.minimum(best, got2[d - 1, 0])
    best_ref[...] = best

    for k in range(views + 1):
        drain(k)
    for side in (0, 1):
        when_sends(side, lambda side=side: halo_copy(side).wait_send())
    swap.wait_send()
    for d in range(1, nx):
        min_copy(d).wait_send()
    for p in range(planes):
        vol_copy(p).wait()


def solution(mesh):
    tiles, nq = mesh.shape["tile"], mesh.shape["plane"]
    nx = nq // 2

    def local(reference_image, source_images, warps, offsets):
        views, planes = warps.shape[0], warps.shape[1]
        part = reference_image.shape[0]
        rows = nq * part
        halves = rows // PART
        vmem = pltpu.VMEM
        dma = pltpu.SemaphoreType.DMA
        scratch = [vmem((3, nx, 2, part, TW), BF16) for _ in range(views)] + [
            vmem((nx, 2, part, TW), BF16),
            vmem((views, planes, 4, TW, TW), BF16),
            vmem((3, rows, TW), BF16),
            vmem((planes, rows, TW), BF16),
            vmem((rows, TW), BF16),
            vmem((3, halves, RUN + 2 * HALF, SUB, TW), F32),
            vmem((planes, halves, RUN, SUB, TW), F32),
            vmem((halves, RUN, SUB, TW), F32),
            vmem((halves, RUN, SUB, TW), F32),
            vmem((4, rows, 128), F32),
            vmem((2, rows, 128), BF16),
            vmem((2, rows, 128), BF16),
            vmem((TW, TW), BF16),
            vmem((TW, TW), BF16),
            vmem((TW, TW), BF16),
            vmem((384, 128), BF16),
            vmem((128, 128), BF16),
            vmem((5, halves, RUN + 2 * HALF, SUB, 128), F32),
            vmem((planes, rows, TW), F32),
            vmem((nx, 2, part, TW), F32),
            vmem((nx, 1, part, TW), F32),
            vmem((nx, 1, part, TW), F32),
            vmem((nx - 1, 1, part, TW), F32),
            dma((views + 1, nx - 1)),
            dma((views + 1, nx - 1)),
            dma((views + 1,)),
            dma((views, 2)),
            dma((views, 2)),
            dma((views + 1, 3)),
            dma((views + 1, 3)),
            dma((views,)),
            dma((2,)),
            dma((2,)),
            dma((nx,)),
            dma((nx,)),
            dma((planes,)),
        ]
        anywhere = pl.BlockSpec(memory_space=pl.ANY)
        return pl.pallas_call(
            functools.partial(body, views, planes, tiles, nq),
            out_shape=(
                jax.ShapeDtypeStruct((planes, rows, TW), F32),
                jax.ShapeDtypeStruct((part, TW), F32),
            ),
            in_specs=[anywhere, anywhere, anywhere, pl.BlockSpec(memory_space=pltpu.SMEM)],
            out_specs=(anywhere, pl.BlockSpec(memory_space=pltpu.VMEM)),
            scratch_shapes=scratch,
            compiler_params=pltpu.CompilerParams(
                collective_id=0, has_side_effects=True, vmem_limit_bytes=58 * 1024 * 1024
            ),
        )(reference_image, source_images, warps, offsets.reshape(-1))

    return jax.shard_map(
        local,
        mesh=mesh,
        in_specs=(
            P("plane", "tile"),
            P(None, "plane", "tile"),
            P(None, "plane", None, None, "tile"),
            P(None, "plane", None, "tile"),
        ),
        out_specs=(P("plane", None, "tile"), P("plane", "tile")),
        check_vma=False,
    )
```

```python
import functools

import jax
import jax.numpy as jnp
from jax import lax
from jax.experimental import pallas as pl
from jax.experimental.pallas import tpu as pltpu
from jax.sharding import PartitionSpec as P

MESH = pl.DeviceIdType.MESH
HALF = 3
COUNT = float((2 * HALF + 1) ** 2)
STABILIZER = 4.0
TW = 256
SUB = 8
RUN = 32
PART = SUB * RUN
EDGE_SLOTS = 8
F32 = jnp.float32
BF16 = jnp.bfloat16


def iota(shape, dim):
    return lax.broadcasted_iota(jnp.int32, shape, dim)


def third(x):
    return (x * 171) >> 9


def as01(mask):
    return jnp.where(mask, 1.0, 0.0).astype(BF16)


def mm(a, b):
    return jnp.dot(a, b, preferred_element_type=F32)


def split2(x):
    hi = x.astype(BF16)
    return hi, (x - hi.astype(F32)).astype(BF16)


def body(
    views,
    planes,
    tiles,
    nq,
    ref_hbm,
    src_hbm,
    warp_hbm,
    off_ref,
    vol,
    best_ref,
    srcs,
    ref_all,
    warp,
    picked,
    wb,
    rb,
    sums_even,
    sums_odd,
    acc,
    rn,
    inv,
    slab,
    cells16,
    halo,
    band,
    perm,
    unperm,
    select,
    edge_t,
    edge_q,
    esums,
    low,
    got1,
    red,
    got2,
    s1_send,
    s1_recv,
    own_sem,
    z_send,
    z_recv,
    f_send,
    f_recv,
    w_sem,
    h_send,
    h_recv,
    p_send,
    p_recv,
    m_send,
    m_recv,
):
    nx = nq // 2
    rows = nq * ref_hbm.shape[0]
    halves = rows // PART
    per = nx // halves
    t = lax.axis_index("tile")
    q = lax.axis_index("plane")
    x = q // 2
    c = q % 2
    sib = 2 * x + 1 - c
    has_left = t > 0
    has_right = t < tiles - 1
    left = lax.rem(t + tiles - 1, tiles)
    right = lax.rem(t + 1, tiles)

    def at_x(d):
        return lax.rem(x + d + nx, nx)

    def remote(src, dst, ssem, rsem, dev):
        return pltpu.make_async_remote_copy(
            src_ref=src,
            dst_ref=dst,
            send_sem=ssem,
            recv_sem=rsem,
            device_id=dev,
            device_id_type=MESH,
        )

    REF = "ref"

    def sem_at(k):
        return views if k is REF else k

    def piece(k):
        return ref_hbm if k is REF else src_hbm.at[k]

    def slot(k, xx, cc):
        return ref_all.at[xx, cc] if k is REF else srcs.at[k, 1, xx, cc]

    def column(k, block, cc):
        if k is REF:
            return ref_all.at[:, pl.ds(cc, 1)]
        return srcs.at[k, block, :, pl.ds(cc, 1)]

    def own_copy(k):
        return pltpu.make_async_copy(piece(k), slot(k, x, c), own_sem.at[sem_at(k)])

    def x_copy(k, d, where):
        n = sem_at(k)
        return remote(
            piece(k), slot(k, where, c), s1_send.at[n, d - 1], s1_recv.at[n, d - 1], (t, 2 * at_x(d) + c)
        )

    def x_send(k, d):
        return x_copy(k, d, x)

    def x_arrival(k, d):
        return x_copy(k, d, at_x(-d))

    def z_copy(k, side):
        return remote(
            column(k, 1, c),
            column(k, 2 * side, c),
            z_send.at[k, side],
            z_recv.at[k, side],
            (right if side == 0 else left, q),
        )

    def sib_copy(k, block, cc):
        n = sem_at(k)
        place = column(k, block, cc)
        return remote(place, place, f_send.at[n, block], f_recv.at[n, block], (t, sib))

    def when_arrives(side, fn):
        pl.when(has_left if side == 0 else has_right)(fn)

    def when_sends(side, fn):
        pl.when(has_right if side == 0 else has_left)(fn)

    def stage1(k):
        for d in range(1, nx):
            x_send(k, d).start()

    def stage2(k):
        own_copy(k).wait()
        for d in range(1, nx):
            x_arrival(k, d).wait_recv()
        if k is not REF:
            for side in (0, 1):
                when_sends(side, lambda side=side: z_copy(k, side).start())
        sib_copy(k, 1, c).start()

    def stage3(k):
        for side in (0, 1):

            @functools.partial(when_arrives, side)
            def _():
                z_copy(k, side).wait_recv()
                sib_copy(k, 2 * side, c).start()

    def finish(k):
        sib_copy(k, 1, 1 - c).wait_recv()
        if k is not REF:
            for side in (0, 1):
                when_arrives(side, lambda side=side: sib_copy(k, 2 * side, 1 - c).wait_recv())

    def drain(k):
        for d in range(1, nx):
            x_send(k, d).wait_send()
        sib_copy(k, 1, c).wait_send()
        if k is not REF:
            for side in (0, 1):
                when_sends(side, lambda side=side: z_copy(k, side).wait_send())
                when_arrives(side, lambda side=side: sib_copy(k, 2 * side, c).wait_send())

    def warp_copy(k):
        return pltpu.make_async_copy(warp_hbm.at[k], warp.at[k], w_sem.at[k])

    def halo_copy(side):
        return remote(
            cells16.at[3 if side == 0 else 0],
            halo.at[side],
            h_send.at[side],
            h_recv.at[side],
            (right if side == 0 else left, q),
        )

    barrier = pltpu.get_barrier_semaphore()
    partners = [(t, 2 * at_x(d) + c) for d in range(1, nx)] + [(t, sib), (left, q), (right, q)]
    for dev in partners:
        pl.semaphore_signal(barrier, inc=1, device_id=dev, device_id_type=MESH)
    for k in [0, REF, *range(1, views)]:
        own_copy(k).start()
    for k in range(views):
        warp_copy(k).start()

    ri, ci = iota((TW, TW), 0), iota((TW, TW), 1)
    band[...] = as01(jnp.abs(ri - ci) <= HALF)
    perm[...] = as01(((ri & (SUB - 1)) * RUN + (ri >> 3)) == ci)
    unperm[...] = as01(((ci & (SUB - 1)) * RUN + (ci >> 3)) == ri)
    rk, cl = iota((384, 128), 0), iota((384, 128), 1)
    kk = rk & 127
    ki, li = third(kk), third(cl)
    gap = (rk >> 7) * 3 - 3 + (kk - 3 * ki) - (cl - 3 * li)
    edge_t[...] = as01((ki == li) & (jnp.abs(gap) <= HALF))
    rq, cq = iota((128, 128), 0), iota((128, 128), 1)
    r_lane = 3 * views * planes
    edge_q[...] = as01(rq == r_lane + cq - 3 * third(cq))
    slabs = slab.shape[0]
    rs, cs = iota((128 * slabs, 512), 0), iota((128 * slabs, 512), 1)
    cl = cs & 127
    ci3 = third(cl)
    spot = jnp.where(cl >= r_lane, EDGE_SLOTS * 12, (ci3 >> 3) * 128 + (ci3 & 7) * 12)
    wanted = spot + ((cs >> 7) ^ 2) * 3 + cl - 3 * ci3
    select[...] = as01((rs == wanted) & (cl < r_lane + 3))
    slab[...] = jnp.zeros_like(slab)
    acc[...] = jnp.zeros_like(acc)
    sums_even[...] = jnp.zeros_like(sums_even)
    wb[planes - 1] = jnp.zeros_like(wb[planes - 1])

    @pl.when(jnp.logical_not(has_left))
    def _():
        halo[0] = jnp.zeros_like(halo[0])
        for k in range(views):
            srcs[k, 0] = jnp.zeros_like(srcs[k, 0])

    @pl.when(jnp.logical_not(has_right))
    def _():
        halo[1] = jnp.zeros_like(halo[1])
        for k in range(views):
            srcs[k, 2] = jnp.zeros_like(srcs[k, 2])

    pl.semaphore_wait(barrier, len(partners))
    for k in [0, REF, *range(1, views)]:
        stage1(k)

    lane = iota((rows, 128), 1)

    def pack(w, n, spot):
        first = 12 * spot
        turned = pltpu.roll(jnp.where(lane < 64, w[:, :128], w[:, 128:]), first + 6, 1)
        slab[n] = jnp.where((lane >= first) & (lane < first + 12), turned, slab[n])

    def permute(value):
        return jnp.concatenate(
            [mm(perm[...], value[PART * h : PART * (h + 1)]).astype(BF16) for h in range(halves)], axis=0
        )

    def put_sums(target, n, value):
        wide = value.shape[1]
        cells = value.reshape(halves, RUN, SUB, wide)
        sub = iota((HALF, SUB, wide), 1)
        target[n, :, HALF : HALF + RUN] = cells
        before = [pltpu.roll(cells[h, RUN - HALF :], 1, 1) for h in range(halves)]
        after = [pltpu.roll(cells[h, :HALF], SUB - 1, 1) for h in range(halves)]
        zero = jnp.zeros((HALF, SUB, wide), F32)
        for h in range(halves):
            target[n, h, :HALF] = jnp.where(sub == 0, before[h - 1] if h else zero, before[h])
            target[n, h, HALF + RUN :] = jnp.where(
                sub == SUB - 1, after[h + 1] if h + 1 < halves else zero, after[h]
            )

    def row_sums(source, n, h, first, size, lanes):
        v = source[n, h, first : first + size + 6, :, lanes]
        two = v[: size + 5] + v[1 : size + 6]
        four = two[:size] + two[2 : size + 2]
        return (four + two[4 : size + 4]) + v[6 : size + 6]

    stage2(0)
    stage2(REF)
    stage2(1)
    if views > 2:
        stage2(2)
    stage3(0)
    finish(REF)

    r = permute(ref_all[...].reshape(rows, TW))
    rb[...] = r
    rf = r.astype(F32)
    pack(rf, 0, EDGE_SLOTS)
    rr_hi, rr_lo = split2(rf * rf)
    put_sums(sums_odd, 0, mm(r, band[...]))
    put_sums(sums_odd, 1, mm(rr_hi, band[...]) + mm(rr_lo, band[...]))
    for h in range(halves):
        sr = row_sums(sums_odd, 0, h, 0, RUN, slice(0, TW))
        srr = row_sums(sums_odd, 1, h, 0, RUN, slice(0, TW))
        mean = sr * (1.0 / COUNT)
        rn[h] = mean
        inv[h] = lax.rsqrt(jnp.maximum(srr - sr * mean, 0.0) + STABILIZER)

    STEP = 16

    def bring(v):
        finish(v)
        warp_copy(v).wait()

    def pick(v):
        for b in range(3):
            picked[b] = permute(srcs[v, b].reshape(rows, TW))

    def resample(v, p):
        blocks = [picked[off_ref[p, s, 0, v] + 1] for s in range(4)]
        w = mm(jnp.concatenate(blocks, axis=1), warp[v, p].reshape(4 * TW, TW))
        wb[p] = w.astype(BF16)
        i = v * planes + p
        pack(w, i // EDGE_SLOTS, i % EDGE_SLOTS)

    buffers = (sums_even, sums_odd)

    def box_columns(p):
        target = buffers[p % 2]
        w = wb[p]
        put_sums(target, 0, mm(w, band[...]))
        put_sums(target, 1, mm(w * w, band[...]))
        put_sums(target, 2, mm(w * rb[...], band[...]))

    def correlate(p):
        source = buffers[p % 2]
        for h in range(halves):
            for first in range(0, RUN, STEP):
                for lanes in (slice(0, 128), slice(128, 256)):
                    sw, sww, srw = [row_sums(source, n, h, first, STEP, lanes) for n in range(3)]
                    here = slice(first, first + STEP)
                    covar = srw - rn[h, here, :, lanes] * sw
                    var = jnp.maximum(sww - sw * (sw * (1.0 / COUNT)), 0.0) + STABILIZER
                    acc[p, h, here, :, lanes] += covar * lax.rsqrt(var)

    def view_step(v, carry):
        pl.when(v + 3 < views)(lambda: stage2(v + 3))
        bring(v)
        pick(v)
        for p in range(planes):
            if p == planes // 2:
                stage3(v + 1)
            resample(v, p)
            box_columns((p - 1) % planes)
            correlate((p - 2) % planes)
        return carry

    last = views - 1
    lax.fori_loop(0, last, view_step, 0)
    bring(last)
    pick(last)
    for p in range(planes):
        resample(last, p)
        if p == 0:
            box_columns(planes - 1)
        if p < 2:
            correlate(planes - 2 + p)
    own = jnp.concatenate([slab[n].astype(BF16) for n in range(slabs)], axis=1)
    for g in range(4):
        cells16[g] = mm(own, select[:, 128 * g : 128 * (g + 1)]).astype(BF16)
    for side in (0, 1):
        when_sends(side, lambda side=side: halo_copy(side).start())
    for p in range(planes):
        box_columns(p)
        if p:
            correlate(p - 1)
    correlate(planes - 1)

    for side in (0, 1):
        when_arrives(side, lambda side=side: halo_copy(side).wait_recv())

    edges = []
    for side in (0, 1):
        cells = [halo[0], cells16[0], cells16[1]] if side == 0 else [cells16[2], cells16[3], halo[1]]
        refs = [mm(cell, edge_q[...]).astype(BF16) for cell in cells]
        w, rw = jnp.concatenate(cells, axis=1), jnp.concatenate(refs, axis=1)
        wf, rf = w.astype(F32), rw.astype(F32)

        def summed(value):
            hi, lo = split2(value)
            return mm(hi, edge_t[...]) + mm(lo, edge_t[...])

        put_sums(esums, 0, mm(w, edge_t[...]))
        put_sums(esums, 1, summed(wf * wf))
        put_sums(esums, 2, summed(rf * wf))
        put_sums(esums, 3, mm(rw, edge_t[...]))
        put_sums(esums, 4, summed(rf * rf))
        out = []
        for h in range(halves):
            sw, sww, srw, sr, srr = [row_sums(esums, n, h, 0, RUN, slice(0, 128)) for n in range(5)]
            covar = srw - sr * (sw * (1.0 / COUNT))
            var = jnp.maximum(sww - sw * (sw * (1.0 / COUNT)), 0.0) + STABILIZER
            var_r = jnp.maximum(srr - sr * (sr * (1.0 / COUNT)), 0.0) + STABILIZER
            ncc = covar * (lax.rsqrt(var) * lax.rsqrt(var_r))
            total = ncc
            for v in range(1, views):
                total = total + pltpu.roll(ncc, 128 - 3 * planes * v, 2)
            out.append(total)
        edges.append(out)

    lane3 = iota((RUN, SUB, 128), 2)

    def swap(h, cc):
        return remote(
            low.at[pl.ds(per * h, per), pl.ds(cc, 1)],
            got1.at[pl.ds(per * h, per)],
            p_send.at[h],
            p_recv.at[h],
            (t, sib),
        )

    for h in range(halves):
        for p in range(planes):
            total = acc[p, h] * inv[h]
            l_edge = pltpu.roll(edges[0][h], (128 - 3 * p) % 128, 2)
            r_edge = pltpu.roll(edges[1][h], 125 - 3 * p, 2)
            total = jnp.concatenate(
                [
                    jnp.where(lane3 < 3, l_edge, total[:, :, :128]),
                    jnp.where(lane3 >= 125, r_edge, total[:, :, 128:]),
                ],
                axis=2,
            )
            hi, lo = split2((total * (1.0 / views)).reshape(PART, TW))
            cost = 1.0 - (mm(unperm[...], hi) + mm(unperm[...], lo))
            vol[p, PART * h : PART * (h + 1)] = cost
            cost4 = cost.reshape(per, 2, rows // nq, TW)
            spot = slice(per * h, per * (h + 1))
            low[spot] = cost4 if p == 0 else jnp.minimum(low[spot], cost4)
        swap(h, 1 - c).start()

    def min_copy(xx, way):
        return remote(red.at[xx], got2.at[way - 1], m_send.at[way], m_recv.at[way], (t, 2 * xx + c))

    for h in range(halves):
        swap(h, 1 - c).wait_recv()
        spot = slice(per * h, per * (h + 1))
        red[spot] = jnp.minimum(low[spot, pl.ds(c, 1)], got1[spot])
        for xx in range(per * h, per * (h + 1)):
            pl.when(x != xx)(lambda xx=xx: min_copy(xx, lax.rem(xx - x + nx, nx)).start())
    for d in range(1, nx):
        min_copy(at_x(d), d).wait_recv()
    best = red[x, 0]
    for d in range(1, nx):
        best = jnp.minimum(best, got2[d - 1, 0])
    best_ref[...] = best

    for k in [REF, *range(views)]:
        drain(k)
    for side in (0, 1):
        when_sends(side, lambda side=side: halo_copy(side).wait_send())
    for h in range(halves):
        swap(h, 1 - c).wait_send()
    for d in range(1, nx):
        min_copy(at_x(d), d).wait_send()


def solution(mesh):
    tiles, nq = mesh.shape["tile"], mesh.shape["plane"]
    nx = nq // 2

    def local(reference_image, source_images, warps, offsets):
        views, planes = warps.shape[0], warps.shape[1]
        part = reference_image.shape[0]
        rows = nq * part
        halves = rows // PART
        slabs = -(-views * planes // EDGE_SLOTS)
        vmem = pltpu.VMEM
        dma = pltpu.SemaphoreType.DMA
        scratch = [
            vmem((views, 3, nx, 2, part, TW), BF16),
            vmem((nx, 2, part, TW), BF16),
            vmem((views, planes, 4, TW, TW), BF16),
            vmem((3, rows, TW), BF16),
            vmem((planes, rows, TW), BF16),
            vmem((rows, TW), BF16),
            vmem((3, halves, RUN + 2 * HALF, SUB, TW), F32),
            vmem((3, halves, RUN + 2 * HALF, SUB, TW), F32),
            vmem((planes, halves, RUN, SUB, TW), F32),
            vmem((halves, RUN, SUB, TW), F32),
            vmem((halves, RUN, SUB, TW), F32),
            vmem((slabs, rows, 128), F32),
            vmem((4, rows, 128), BF16),
            vmem((2, rows, 128), BF16),
            vmem((TW, TW), BF16),
            vmem((TW, TW), BF16),
            vmem((TW, TW), BF16),
            vmem((128 * slabs, 512), BF16),
            vmem((384, 128), BF16),
            vmem((128, 128), BF16),
            vmem((5, halves, RUN + 2 * HALF, SUB, 128), F32),
            vmem((nx, 2, part, TW), F32),
            vmem((nx, 1, part, TW), F32),
            vmem((nx, 1, part, TW), F32),
            vmem((nx - 1, 1, part, TW), F32),
            dma((views + 1, nx - 1)),
            dma((views + 1, nx - 1)),
            dma((views + 1,)),
            dma((views, 2)),
            dma((views, 2)),
            dma((views + 1, 3)),
            dma((views + 1, 3)),
            dma((views,)),
            dma((2,)),
            dma((2,)),
            dma((halves,)),
            dma((halves,)),
            dma((nx,)),
            dma((nx,)),
        ]
        far = pl.BlockSpec(memory_space=pltpu.HBM)
        near = pl.BlockSpec(memory_space=pltpu.VMEM)
        return pl.pallas_call(
            functools.partial(body, views, planes, tiles, nq),
            out_shape=(pltpu.VMEM((planes, rows, TW), F32), pltpu.VMEM((part, TW), F32)),
            in_specs=[far, far, far, pl.BlockSpec(memory_space=pltpu.SMEM)],
            out_specs=(near, near),
            scratch_shapes=scratch,
            compiler_params=pltpu.CompilerParams(
                collective_id=0, has_side_effects=True, vmem_limit_bytes=63300 * 1024
            ),
        )(reference_image, source_images, warps, offsets.transpose(1, 2, 3, 0))

    return jax.shard_map(
        local,
        mesh=mesh,
        in_specs=(
            P("plane", "tile"),
            P(None, "plane", "tile"),
            P(None, "plane", None, None, "tile"),
            P(None, "plane", None, "tile"),
        ),
        out_specs=(P("plane", None, "tile"), P("plane", "tile")),
        check_vma=False,
    )
```

```python
import functools

import jax
import jax.numpy as jnp
from jax import lax
from jax.experimental import pallas as pl
from jax.experimental.pallas import tpu as pltpu
from jax.sharding import PartitionSpec as P

MESH = pl.DeviceIdType.MESH
HALF = 3
COUNT = float((2 * HALF + 1) ** 2)
STABILIZER = 4.0
TW = 256
SUB = 8
RUN = 32
PART = SUB * RUN
EDGE_SLOTS = 8
F32 = jnp.float32
BF16 = jnp.bfloat16


def iota(shape, dim):
    return lax.broadcasted_iota(jnp.int32, shape, dim)


def third(x):
    return (x * 171) >> 9


def as01(mask):
    return jnp.where(mask, 1.0, 0.0).astype(BF16)


def mm(a, b):
    return jnp.dot(a, b, preferred_element_type=F32)


def split2(x):
    hi = x.astype(BF16)
    return hi, (x - hi.astype(F32)).astype(BF16)


def body(
    views,
    planes,
    tiles,
    nq,
    ref_hbm,
    src_hbm,
    warp_hbm,
    off_ref,
    vol,
    best_ref,
    srcs,
    ref_all,
    warp,
    picked,
    wb,
    rb,
    sums_even,
    sums_odd,
    acc,
    rn,
    inv,
    slab,
    cells16,
    halo,
    band,
    perm,
    unperm,
    select,
    edge_t,
    edge_q,
    esums,
    eparts,
    low,
    got1,
    red,
    got2,
    emin,
    egot,
    etall,
    s1_send,
    s1_recv,
    own_sem,
    z_send,
    z_recv,
    y_send,
    y_recv,
    f_send,
    f_recv,
    w_sem,
    h_send,
    h_recv,
    p_send,
    p_recv,
    m_send,
    m_recv,
    e_send,
    e_recv,
):
    nx = nq // 2
    zviews = views - views // 3
    rows = nq * ref_hbm.shape[0]
    halves = rows // PART
    per = nx // halves
    t = lax.axis_index("tile")
    q = lax.axis_index("plane")
    x = q // 2
    c = q % 2
    sib = 2 * x + 1 - c
    has_left = t > 0
    has_right = t < tiles - 1
    left = lax.rem(t + tiles - 1, tiles)
    right = lax.rem(t + 1, tiles)

    def at_x(d):
        return lax.rem(x + d + nx, nx)

    def remote(src, dst, ssem, rsem, dev):
        return pltpu.make_async_remote_copy(
            src_ref=src,
            dst_ref=dst,
            send_sem=ssem,
            recv_sem=rsem,
            device_id=dev,
            device_id_type=MESH,
        )

    REF = "ref"

    def sem_at(k):
        return views if k is REF else k

    def piece(k):
        return ref_hbm if k is REF else src_hbm.at[k]

    def slot(k, xx, cc):
        return ref_all.at[xx, cc] if k is REF else srcs.at[k, 1, xx, cc]

    def column(k, block, cc):
        if k is REF:
            return ref_all.at[:, pl.ds(cc, 1)]
        return srcs.at[k, block, :, pl.ds(cc, 1)]

    def own_copy(k):
        return pltpu.make_async_copy(piece(k), slot(k, x, c), own_sem.at[sem_at(k)])

    def x_copy(k, d, where):
        n = sem_at(k)
        return remote(
            piece(k), slot(k, where, c), s1_send.at[n, d - 1], s1_recv.at[n, d - 1], (t, 2 * at_x(d) + c)
        )

    def x_send(k, d):
        return x_copy(k, d, x)

    def x_arrival(k, d):
        return x_copy(k, d, at_x(-d))

    def z_copy(k, side):
        return remote(
            column(k, 1, c),
            column(k, 2 * side, c),
            z_send.at[k, side],
            z_recv.at[k, side],
            (right if side == 0 else left, q),
        )

    def raw_copy(k, side):
        return remote(
            piece(k), slot2(k, side, x), z_send.at[k, side], z_recv.at[k, side], (right if side == 0 else left, q)
        )

    def slot2(k, side, xx):
        return srcs.at[k, 2 * side, xx, c]

    def y_copy(k, side, d, where):
        place = slot2(k, side, where)
        n = k - zviews
        return remote(
            place, place, y_send.at[n, side, d - 1], y_recv.at[n, side, d - 1], (t, 2 * at_x(d) + c)
        )

    def sib_copy(k, block, cc):
        n = sem_at(k)
        place = column(k, block, cc)
        return remote(place, place, f_send.at[n, block], f_recv.at[n, block], (t, sib))

    def when_arrives(side, fn):
        pl.when(has_left if side == 0 else has_right)(fn)

    def when_sends(side, fn):
        pl.when(has_right if side == 0 else has_left)(fn)

    def stage1(k):
        for d in range(1, nx):
            x_send(k, d).start()

    def stage2(k):
        own_copy(k).wait()
        for d in range(1, nx):
            x_arrival(k, d).wait_recv()
        if k is not REF:

            @pl.when(k < zviews)
            def _():
                for side in (0, 1):
                    when_sends(side, lambda side=side: z_copy(k, side).start())

        sib_copy(k, 1, c).start()

    def pass_on(k):
        for side in (0, 1):

            @functools.partial(when_arrives, side)
            def _():
                raw_copy(k, side).wait_recv()
                for d in range(1, nx):
                    y_copy(k, side, d, x).start()

    def stage3(k):
        for side in (0, 1):

            @functools.partial(when_arrives, side)
            def _():
                @pl.when(k < zviews)
                def _():
                    z_copy(k, side).wait_recv()

                @pl.when(k >= zviews)
                def _():
                    for d in range(1, nx):
                        y_copy(k, side, d, at_x(-d)).wait_recv()

                sib_copy(k, 2 * side, c).start()

    def finish(k):
        sib_copy(k, 1, 1 - c).wait_recv()
        if k is not REF:
            for side in (0, 1):
                when_arrives(side, lambda side=side: sib_copy(k, 2 * side, 1 - c).wait_recv())

    def drain(k):
        for d in range(1, nx):
            x_send(k, d).wait_send()
        sib_copy(k, 1, c).wait_send()
        if k is not REF:
            for side in (0, 1):
                late = k >= zviews
                copy = raw_copy if late else z_copy
                when_sends(side, lambda side=side, copy=copy: copy(k, side).wait_send())
                when_arrives(side, lambda side=side: sib_copy(k, 2 * side, c).wait_send())
                for d in range(1, nx if late else 1):
                    when_arrives(side, lambda side=side, d=d: y_copy(k, side, d, x).wait_send())

    def warp_copy(k):
        return pltpu.make_async_copy(warp_hbm.at[k], warp.at[k], w_sem.at[k])

    def halo_copy(side):
        return remote(
            cells16.at[3 if side == 0 else 0],
            halo.at[side],
            h_send.at[side],
            h_recv.at[side],
            (right if side == 0 else left, q),
        )

    barrier = pltpu.get_barrier_semaphore()
    partners = [(t, 2 * at_x(d) + c) for d in range(1, nx)] + [(t, sib), (left, q), (right, q)]
    partners += [(t, 2 * at_x(d) + 1 - c) for d in range(1, nx)]
    for dev in partners:
        pl.semaphore_signal(barrier, inc=1, device_id=dev, device_id_type=MESH)
    for k in [0, REF, *range(1, views)]:
        own_copy(k).start()
    for k in range(views):
        warp_copy(k).start()

    ri, ci = iota((TW, TW), 0), iota((TW, TW), 1)
    band[...] = as01(jnp.abs(ri - ci) <= HALF)
    perm[...] = as01(((ri & (SUB - 1)) * RUN + (ri >> 3)) == ci)
    unperm[...] = as01(((ci & (SUB - 1)) * RUN + (ci >> 3)) == ri)
    rk, cl = iota((384, 128), 0), iota((384, 128), 1)
    kk = rk & 127
    ki, li = third(kk), third(cl)
    gap = (rk >> 7) * 3 - 3 + (kk - 3 * ki) - (cl - 3 * li)
    edge_t[...] = as01((ki == li) & (jnp.abs(gap) <= HALF))
    rq, cq = iota((128, 128), 0), iota((128, 128), 1)
    r_lane = 3 * views * planes
    edge_q[...] = as01(rq == r_lane + cq - 3 * third(cq))
    slabs = slab.shape[0]
    rs, cs = iota((128 * slabs, 512), 0), iota((128 * slabs, 512), 1)
    cl = cs & 127
    ci3 = third(cl)
    spot = jnp.where(cl >= r_lane, EDGE_SLOTS * 12, (ci3 >> 3) * 128 + (ci3 & 7) * 12)
    wanted = spot + ((cs >> 7) ^ 2) * 3 + cl - 3 * ci3
    select[...] = as01((rs == wanted) & (cl < r_lane + 3))
    slab[...] = jnp.zeros_like(slab)
    acc[...] = jnp.zeros_like(acc)
    sums_even[...] = jnp.zeros_like(sums_even)
    wb[planes - 1] = jnp.zeros_like(wb[planes - 1])

    @pl.when(jnp.logical_not(has_left))
    def _():
        halo[0] = jnp.zeros_like(halo[0])
        for k in range(views):
            srcs[k, 0] = jnp.zeros_like(srcs[k, 0])

    @pl.when(jnp.logical_not(has_right))
    def _():
        halo[1] = jnp.zeros_like(halo[1])
        for k in range(views):
            srcs[k, 2] = jnp.zeros_like(srcs[k, 2])

    pl.semaphore_wait(barrier, len(partners))
    stage1(0)
    for k in range(zviews, views):
        for side in (0, 1):
            when_sends(side, lambda side=side, k=k: raw_copy(k, side).start())
    for k in [REF, *range(1, views)]:
        stage1(k)

    lane = iota((rows, 128), 1)

    def pack(w, n, spot):
        first = 12 * spot
        turned = pltpu.roll(jnp.where(lane < 64, w[:, :128], w[:, 128:]), first + 6, 1)
        slab[n] = jnp.where((lane >= first) & (lane < first + 12), turned, slab[n])

    def permute(value):
        return jnp.concatenate(
            [mm(perm[...], value[PART * h : PART * (h + 1)]).astype(BF16) for h in range(halves)], axis=0
        )

    def put_sums(target, n, value):
        wide = value.shape[1]
        cells = value.reshape(halves, RUN, SUB, wide)
        sub = iota((HALF, SUB, wide), 1)
        target[n, :, HALF : HALF + RUN] = cells
        before = [pltpu.roll(cells[h, RUN - HALF :], 1, 1) for h in range(halves)]
        after = [pltpu.roll(cells[h, :HALF], SUB - 1, 1) for h in range(halves)]
        zero = jnp.zeros((HALF, SUB, wide), F32)
        for h in range(halves):
            target[n, h, :HALF] = jnp.where(sub == 0, before[h - 1] if h else zero, before[h])
            target[n, h, HALF + RUN :] = jnp.where(
                sub == SUB - 1, after[h + 1] if h + 1 < halves else zero, after[h]
            )

    def row_sums(source, n, h, first, size, lanes):
        v = source[n, h, first : first + size + 6, :, lanes]
        two = v[: size + 5] + v[1 : size + 6]
        four = two[:size] + two[2 : size + 2]
        return (four + two[4 : size + 4]) + v[6 : size + 6]

    stage2(0)
    stage2(REF)
    stage2(1)
    if views > 2:
        stage2(2)
    stage3(0)
    for k in range(zviews, views):
        pass_on(k)
    finish(REF)

    r = permute(ref_all[...].reshape(rows, TW))
    rb[...] = r
    rf = r.astype(F32)
    pack(rf, 0, EDGE_SLOTS)
    rr_hi, rr_lo = split2(rf * rf)
    put_sums(sums_odd, 0, mm(r, band[...]))
    put_sums(sums_odd, 1, mm(rr_hi, band[...]) + mm(rr_lo, band[...]))
    for h in range(halves):
        sr = row_sums(sums_odd, 0, h, 0, RUN, slice(0, TW))
        srr = row_sums(sums_odd, 1, h, 0, RUN, slice(0, TW))
        mean = sr * (1.0 / COUNT)
        rn[h] = mean
        inv[h] = lax.rsqrt(jnp.maximum(srr - sr * mean, 0.0) + STABILIZER)

    STEP = 16

    def bring(v):
        finish(v)
        warp_copy(v).wait()

    def pick(v):
        for b in range(3):
            picked[b] = permute(srcs[v, b].reshape(rows, TW))

    def resample(v, p):
        blocks = [picked[off_ref[p, s, 0, v] + 1] for s in range(4)]
        w = mm(jnp.concatenate(blocks, axis=1), warp[v, p].reshape(4 * TW, TW))
        wb[p] = w.astype(BF16)
        i = v * planes + p
        pack(w, i // EDGE_SLOTS, i % EDGE_SLOTS)

    buffers = (sums_even, sums_odd)

    def box_columns(p):
        target = buffers[p % 2]
        w = wb[p]
        put_sums(target, 0, mm(w, band[...]))
        put_sums(target, 1, mm(w * w, band[...]))
        put_sums(target, 2, mm(w * rb[...], band[...]))

    def correlate(p):
        source = buffers[p % 2]
        for h in range(halves):
            for first in range(0, RUN, STEP):
                for lanes in (slice(0, 128), slice(128, 256)):
                    sw, sww, srw = [row_sums(source, n, h, first, STEP, lanes) for n in range(3)]
                    here = slice(first, first + STEP)
                    covar = srw - rn[h, here, :, lanes] * sw
                    var = jnp.maximum(sww - sw * (sw * (1.0 / COUNT)), 0.0) + STABILIZER
                    acc[p, h, here, :, lanes] += covar * lax.rsqrt(var)

    def view_step(v, carry):
        pl.when(v + 3 < views)(lambda: stage2(v + 3))
        bring(v)
        pick(v)
        for p in range(planes):
            if p == planes // 2:
                stage3(v + 1)
            resample(v, p)
            box_columns((p - 1) % planes)
            correlate((p - 2) % planes)
        return carry

    last = views - 1
    lax.fori_loop(0, last, view_step, 0)
    bring(last)
    pick(last)
    for p in range(planes):
        resample(last, p)
        if p == 0:
            box_columns(planes - 1)
        if p < 2:
            correlate(planes - 2 + p)
    own = jnp.concatenate([slab[n].astype(BF16) for n in range(slabs)], axis=1)
    for g in range(4):
        cells16[g] = mm(own, select[:, 128 * g : 128 * (g + 1)]).astype(BF16)
    for side in (0, 1):
        when_sends(side, lambda side=side: halo_copy(side).start())
    for p in range(planes):
        box_columns(p)
        if p:
            correlate(p - 1)
    correlate(planes - 1)

    def edge_terms(cells, taps):
        refs = [mm(cell, edge_q[...]).astype(BF16) for cell in cells]
        w, rw = jnp.concatenate(cells, axis=1), jnp.concatenate(refs, axis=1)
        wf, rf = w.astype(F32), rw.astype(F32)

        def summed(value):
            hi, lo = split2(value)
            return mm(hi, taps) + mm(lo, taps)

        return [mm(w, taps), summed(wf * wf), summed(rf * wf), mm(rw, taps), summed(rf * rf)]

    for side in (0, 1):
        taps = edge_t[128:] if side == 0 else edge_t[:256]
        for n, term in enumerate(edge_terms([cells16[2 * side], cells16[2 * side + 1]], taps)):
            eparts[side, n] = term

    def in_order(value):
        hi, lo = split2(value * (1.0 / views))
        return 1.0 - (mm(unperm[...], hi) + mm(unperm[...], lo))

    for h in range(halves):
        for p in range(planes):
            cost = in_order((acc[p, h] * inv[h]).reshape(PART, TW))
            vol[p, PART * h : PART * (h + 1)] = cost
            cost4 = cost.reshape(per, 2, rows // nq, TW)
            spot = slice(per * h, per * (h + 1))
            low[spot] = cost4 if p == 0 else jnp.minimum(low[spot], cost4)

    def swap(h, cc):
        return remote(
            low.at[pl.ds(per * h, per), pl.ds(cc, 1)],
            got1.at[pl.ds(per * h, per)],
            p_send.at[h],
            p_recv.at[h],
            (t, sib),
        )

    def min_copy(xx, way):
        return remote(red.at[xx], got2.at[way - 1], m_send.at[way], m_recv.at[way], (t, 2 * xx + c))

    for h in range(halves):
        swap(h, 1 - c).start()

    for side in (0, 1):
        when_arrives(side, lambda side=side: halo_copy(side).wait_recv())
    for h in range(halves):
        swap(h, 1 - c).wait_recv()
    red[...] = jnp.minimum(low[:, pl.ds(c, 1)], got1[...])
    for d in range(1, nx):
        min_copy(at_x(d), d).start()

    edges = []
    for side in (0, 1):
        taps = edge_t[:128] if side == 0 else edge_t[256:]
        for n, term in enumerate(edge_terms([halo[side]], taps)):
            put_sums(esums.at[side], n, eparts[side, n] + term)
        out = []
        for h in range(halves):
            sw, sww, srw, sr, srr = [row_sums(esums.at[side], n, h, 0, RUN, slice(0, 128)) for n in range(5)]
            covar = srw - sr * (sw * (1.0 / COUNT))
            var = jnp.maximum(sww - sw * (sw * (1.0 / COUNT)), 0.0) + STABILIZER
            var_r = jnp.maximum(srr - sr * (sr * (1.0 / COUNT)), 0.0) + STABILIZER
            ncc = covar * (lax.rsqrt(var) * lax.rsqrt(var_r))
            total = ncc
            for v in range(1, views):
                total = total + pltpu.roll(ncc, 128 - 3 * planes * v, 2)
            out.append(in_order(total.reshape(PART, 128)))
        edges.append(out)

    lane2 = iota((PART, 128), 1)
    chip = rows // nx
    for h in range(halves):
        here = slice(PART * h, PART * (h + 1))
        both = []
        for side in (0, 1):
            least = None
            for p in range(planes):
                turned = pltpu.roll(edges[side][h], 125 - 3 * p if side else (128 - 3 * p) % 128, 1)
                least = turned if least is None else jnp.minimum(least, turned)
            both.append(least)
        sides = pltpu.roll(jnp.where(lane2 < 64, both[0], both[1]), 3, 1)
        flat = sides.T
        for n in range(per):
            emin[per * h + n] = flat[:SUB, chip * n : chip * (n + 1)]

    def side_copy(dx, dc):
        n = 2 * dx + dc - 1
        return remote(
            emin.at[at_x(dx)],
            egot.at[n],
            e_send.at[n],
            e_recv.at[n],
            (t, 2 * at_x(dx) + (1 - c if dc else c)),
        )

    others = [(dx, dc) for dx in range(nx) for dc in (0, 1) if dx or dc]
    for dx, dc in others:
        side_copy(dx, dc).start()

    for h in range(halves):
        here = slice(PART * h, PART * (h + 1))
        for side in (0, 1):
            lanes = slice(128 * side, 128 * (side + 1))
            inside = (lane2 >= 125) if side else (lane2 < 3)
            for p in range(planes):
                turned = pltpu.roll(edges[side][h], 125 - 3 * p if side else (128 - 3 * p) % 128, 1)
                vol[p, here, lanes] = jnp.where(inside, turned, vol[p, here, lanes])

    for k in [REF, *range(views)]:
        drain(k)
    for side in (0, 1):
        when_sends(side, lambda side=side: halo_copy(side).wait_send())
    for h in range(halves):
        swap(h, 1 - c).wait_send()

    for d in range(1, nx):
        min_copy(at_x(d), d).wait_recv()
    best = red[x, 0]
    for d in range(1, nx):
        best = jnp.minimum(best, got2[d - 1, 0])
    least = emin[x]
    for dx, dc in others:
        side_copy(dx, dc).wait_recv()
    for dx, dc in others:
        least = jnp.minimum(least, egot[2 * dx + dc - 1])
    part = rows // nq
    etall[...] = jnp.concatenate([least, jnp.zeros((128 - SUB, chip), F32)], axis=0).T
    sides = etall[pl.ds(pl.multiple_of(c * part, part), part)]
    lane1 = iota((part, 128), 1)
    best_ref[:, :128] = jnp.where(lane1 < 3, pltpu.roll(sides, 125, 1), best[:, :128])
    best_ref[:, 128:] = jnp.where(lane1 >= 125, pltpu.roll(sides, 125, 1), best[:, 128:])

    for d in range(1, nx):
        min_copy(at_x(d), d).wait_send()
    for dx, dc in others:
        side_copy(dx, dc).wait_send()


def solution(mesh):
    tiles, nq = mesh.shape["tile"], mesh.shape["plane"]
    nx = nq // 2

    def local(reference_image, source_images, warps, offsets):
        views, planes = warps.shape[0], warps.shape[1]
        part = reference_image.shape[0]
        rows = nq * part
        halves = rows // PART
        slabs = -(-views * planes // EDGE_SLOTS)
        vmem = pltpu.VMEM
        dma = pltpu.SemaphoreType.DMA
        scratch = [
            vmem((views, 3, nx, 2, part, TW), BF16),
            vmem((nx, 2, part, TW), BF16),
            vmem((views, planes, 4, TW, TW), BF16),
            vmem((3, rows, TW), BF16),
            vmem((planes, rows, TW), BF16),
            vmem((rows, TW), BF16),
            vmem((3, halves, RUN + 2 * HALF, SUB, TW), F32),
            vmem((3, halves, RUN + 2 * HALF, SUB, TW), F32),
            vmem((planes, halves, RUN, SUB, TW), F32),
            vmem((halves, RUN, SUB, TW), F32),
            vmem((halves, RUN, SUB, TW), F32),
            vmem((slabs, rows, 128), F32),
            vmem((4, rows, 128), BF16),
            vmem((2, rows, 128), BF16),
            vmem((TW, TW), BF16),
            vmem((TW, TW), BF16),
            vmem((TW, TW), BF16),
            vmem((128 * slabs, 512), BF16),
            vmem((384, 128), BF16),
            vmem((128, 128), BF16),
            vmem((2, 5, halves, RUN + 2 * HALF, SUB, 128), F32),
            vmem((2, 5, rows, 128), F32),
            vmem((nx, 2, part, TW), F32),
            vmem((nx, 1, part, TW), F32),
            vmem((nx, 1, part, TW), F32),
            vmem((nx - 1, 1, part, TW), F32),
            vmem((nx, SUB, 2 * part), F32),
            vmem((nq - 1, SUB, 2 * part), F32),
            vmem((2 * part, 128), F32),
            dma((views + 1, nx - 1)),
            dma((views + 1, nx - 1)),
            dma((views + 1,)),
            dma((views, 2)),
            dma((views, 2)),
            dma((views // 3, 2, nx - 1)),
            dma((views // 3, 2, nx - 1)),
            dma((views + 1, 3)),
            dma((views + 1, 3)),
            dma((views,)),
            dma((2,)),
            dma((2,)),
            dma((halves,)),
            dma((halves,)),
            dma((nx,)),
            dma((nx,)),
            dma((nq - 1,)),
            dma((nq - 1,)),
        ]
        far = pl.BlockSpec(memory_space=pltpu.HBM)
        near = pl.BlockSpec(memory_space=pltpu.VMEM)
        return pl.pallas_call(
            functools.partial(body, views, planes, tiles, nq),
            out_shape=(pltpu.VMEM((planes, rows, TW), F32), pltpu.VMEM((part, TW), F32)),
            in_specs=[far, far, far, pl.BlockSpec(memory_space=pltpu.SMEM)],
            out_specs=(near, near),
            scratch_shapes=scratch,
            compiler_params=pltpu.CompilerParams(
                collective_id=0, has_side_effects=True, vmem_limit_bytes=63300 * 1024
            ),
        )(reference_image, source_images, warps, offsets.transpose(1, 2, 3, 0))

    return jax.shard_map(
        local,
        mesh=mesh,
        in_specs=(
            P("plane", "tile"),
            P(None, "plane", "tile"),
            P(None, "plane", None, None, "tile"),
            P(None, "plane", None, "tile"),
        ),
        out_specs=(P("plane", None, "tile"), P("plane", "tile")),
        check_vma=False,
    )
```

```python
import functools

import jax
import jax.numpy as jnp
from jax import lax
from jax.experimental import pallas as pl
from jax.experimental.pallas import tpu as pltpu
from jax.sharding import PartitionSpec as P

MESH = pl.DeviceIdType.MESH
HALF = 3
COUNT = float((2 * HALF + 1) ** 2)
STABILIZER = 4.0
TW = 256
SUB = 8
RUN = 32
PART = SUB * RUN
EDGE_SLOTS = 8
F32 = jnp.float32
BF16 = jnp.bfloat16


def iota(shape, dim):
    return lax.broadcasted_iota(jnp.int32, shape, dim)


def third(x):
    return (x * 171) >> 9


def as01(mask):
    return jnp.where(mask, 1.0, 0.0).astype(BF16)


def mm(a, b):
    return jnp.dot(a, b, preferred_element_type=F32)


def split2(x):
    hi = x.astype(BF16)
    return hi, (x - hi.astype(F32)).astype(BF16)


def body(
    views,
    planes,
    tiles,
    nq,
    ref_hbm,
    src_hbm,
    warp_hbm,
    off_ref,
    vol,
    best_ref,
    srcs,
    ref_all,
    warp,
    picked,
    wb,
    rb,
    sums_even,
    sums_odd,
    acc,
    rn,
    inv,
    slab,
    cells16,
    halo,
    band,
    perm,
    unperm,
    select,
    edge_t,
    edge_q,
    esums,
    eparts,
    low,
    got1,
    red,
    got2,
    emin,
    egot,
    etall,
    s1_send,
    s1_recv,
    own_sem,
    z_send,
    z_recv,
    y_send,
    y_recv,
    f_send,
    f_recv,
    w_sem,
    h_send,
    h_recv,
    p_send,
    p_recv,
    m_send,
    m_recv,
    e_send,
    e_recv,
):
    nx = nq // 2
    zviews = views - views // 6
    rows = nq * ref_hbm.shape[0]
    halves = rows // PART
    per = nx // halves
    t = lax.axis_index("tile")
    q = lax.axis_index("plane")
    x = q // 2
    c = q % 2
    sib = 2 * x + 1 - c
    has_left = t > 0
    has_right = t < tiles - 1
    left = lax.rem(t + tiles - 1, tiles)
    right = lax.rem(t + 1, tiles)

    def at_x(d):
        return lax.rem(x + d + nx, nx)

    def remote(src, dst, ssem, rsem, dev):
        return pltpu.make_async_remote_copy(
            src_ref=src,
            dst_ref=dst,
            send_sem=ssem,
            recv_sem=rsem,
            device_id=dev,
            device_id_type=MESH,
        )

    REF = "ref"

    def sem_at(k):
        return views if k is REF else k

    def piece(k):
        return ref_hbm if k is REF else src_hbm.at[k]

    def slot(k, xx, cc):
        return ref_all.at[xx, cc] if k is REF else srcs.at[k, 1, xx, cc]

    def column(k, block, cc):
        if k is REF:
            return ref_all.at[:, pl.ds(cc, 1)]
        return srcs.at[k, block, :, pl.ds(cc, 1)]

    def own_copy(k):
        return pltpu.make_async_copy(piece(k), slot(k, x, c), own_sem.at[sem_at(k)])

    def x_copy(k, d, where):
        n = sem_at(k)
        return remote(
            piece(k), slot(k, where, c), s1_send.at[n, d - 1], s1_recv.at[n, d - 1], (t, 2 * at_x(d) + c)
        )

    def x_send(k, d):
        return x_copy(k, d, x)

    def x_arrival(k, d):
        return x_copy(k, d, at_x(-d))

    def z_copy(k, side):
        return remote(
            column(k, 1, c),
            column(k, 2 * side, c),
            z_send.at[k, side],
            z_recv.at[k, side],
            (right if side == 0 else left, q),
        )

    def raw_copy(k, side):
        return remote(
            piece(k), slot2(k, side, x), z_send.at[k, side], z_recv.at[k, side], (right if side == 0 else left, q)
        )

    def slot2(k, side, xx):
        return srcs.at[k, 2 * side, xx, c]

    def y_copy(k, side, d, where):
        place = slot2(k, side, where)
        n = k - zviews
        return remote(
            place, place, y_send.at[n, side, d - 1], y_recv.at[n, side, d - 1], (t, 2 * at_x(d) + c)
        )

    def sib_copy(k, block, cc):
        n = sem_at(k)
        place = column(k, block, cc)
        return remote(place, place, f_send.at[n, block], f_recv.at[n, block], (t, sib))

    def when_arrives(side, fn):
        pl.when(has_left if side == 0 else has_right)(fn)

    def when_sends(side, fn):
        pl.when(has_right if side == 0 else has_left)(fn)

    def stage1(k):
        for d in range(1, nx):
            x_send(k, d).start()

    def stage2(k):
        own_copy(k).wait()
        for d in range(1, nx):
            x_arrival(k, d).wait_recv()
        if k is not REF:

            @pl.when(k < zviews)
            def _():
                for side in (0, 1):
                    when_sends(side, lambda side=side: z_copy(k, side).start())

        sib_copy(k, 1, c).start()

    def pass_on(k):
        for side in (0, 1):

            @functools.partial(when_arrives, side)
            def _():
                raw_copy(k, side).wait_recv()
                for d in range(1, nx):
                    y_copy(k, side, d, x).start()

    def stage3(k):
        for side in (0, 1):

            @functools.partial(when_arrives, side)
            def _():
                @pl.when(k < zviews)
                def _():
                    z_copy(k, side).wait_recv()

                @pl.when(k >= zviews)
                def _():
                    for d in range(1, nx):
                        y_copy(k, side, d, at_x(-d)).wait_recv()

                sib_copy(k, 2 * side, c).start()

    def finish(k):
        sib_copy(k, 1, 1 - c).wait_recv()
        if k is not REF:
            for side in (0, 1):
                when_arrives(side, lambda side=side: sib_copy(k, 2 * side, 1 - c).wait_recv())

    def drain(k):
        for d in range(1, nx):
            x_send(k, d).wait_send()
        sib_copy(k, 1, c).wait_send()
        if k is not REF:
            for side in (0, 1):
                late = k >= zviews
                copy = raw_copy if late else z_copy
                when_sends(side, lambda side=side, copy=copy: copy(k, side).wait_send())
                when_arrives(side, lambda side=side: sib_copy(k, 2 * side, c).wait_send())
                for d in range(1, nx if late else 1):
                    when_arrives(side, lambda side=side, d=d: y_copy(k, side, d, x).wait_send())

    def warp_copy(k):
        return pltpu.make_async_copy(warp_hbm.at[k], warp.at[k], w_sem.at[k])

    def halo_copy(side):
        return remote(
            cells16.at[3 if side == 0 else 0],
            halo.at[side],
            h_send.at[side],
            h_recv.at[side],
            (right if side == 0 else left, q),
        )

    barrier = pltpu.get_barrier_semaphore()
    partners = [(t, 2 * at_x(d) + c) for d in range(1, nx)] + [(t, sib), (left, q), (right, q)]
    partners += [(t, 2 * at_x(d) + 1 - c) for d in range(1, nx)]
    for dev in partners:
        pl.semaphore_signal(barrier, inc=1, device_id=dev, device_id_type=MESH)
    for k in [0, REF, *range(1, views)]:
        own_copy(k).start()
    for k in range(views):
        warp_copy(k).start()

    ri, ci = iota((TW, TW), 0), iota((TW, TW), 1)
    band[...] = as01(jnp.abs(ri - ci) <= HALF)
    perm[...] = as01(((ri & (SUB - 1)) * RUN + (ri >> 3)) == ci)
    unperm[...] = as01(((ci & (SUB - 1)) * RUN + (ci >> 3)) == ri)
    rk, cl = iota((384, 128), 0), iota((384, 128), 1)
    kk = rk & 127
    ki, li = third(kk), third(cl)
    gap = (rk >> 7) * 3 - 3 + (kk - 3 * ki) - (cl - 3 * li)
    edge_t[...] = as01((ki == li) & (jnp.abs(gap) <= HALF))
    rq, cq = iota((128, 128), 0), iota((128, 128), 1)
    r_lane = 3 * views * planes
    edge_q[...] = as01(rq == r_lane + cq - 3 * third(cq))
    slabs = slab.shape[0]
    rs, cs = iota((128 * slabs, 512), 0), iota((128 * slabs, 512), 1)
    cl = cs & 127
    ci3 = third(cl)
    spot = jnp.where(cl >= r_lane, EDGE_SLOTS * 12, (ci3 >> 3) * 128 + (ci3 & 7) * 12)
    wanted = spot + ((cs >> 7) ^ 2) * 3 + cl - 3 * ci3
    select[...] = as01((rs == wanted) & (cl < r_lane + 3))
    slab[...] = jnp.zeros_like(slab)
    acc[...] = jnp.zeros_like(acc)
    sums_even[...] = jnp.zeros_like(sums_even)
    wb[planes - 1] = jnp.zeros_like(wb[planes - 1])

    @pl.when(jnp.logical_not(has_left))
    def _():
        halo[0] = jnp.zeros_like(halo[0])
        for k in range(views):
            srcs[k, 0] = jnp.zeros_like(srcs[k, 0])

    @pl.when(jnp.logical_not(has_right))
    def _():
        halo[1] = jnp.zeros_like(halo[1])
        for k in range(views):
            srcs[k, 2] = jnp.zeros_like(srcs[k, 2])

    pl.semaphore_wait(barrier, len(partners))
    stage1(0)
    for k in range(zviews, views):
        for side in (0, 1):
            when_sends(side, lambda side=side, k=k: raw_copy(k, side).start())
    for k in [REF, *range(1, views)]:
        stage1(k)

    lane = iota((rows, 128), 1)

    def pack(w, n, spot):
        first = 12 * spot
        turned = pltpu.roll(jnp.where(lane < 64, w[:, :128], w[:, 128:]), first + 6, 1)
        slab[n] = jnp.where((lane >= first) & (lane < first + 12), turned, slab[n])

    def permute(value):
        return jnp.concatenate(
            [mm(perm[...], value[PART * h : PART * (h + 1)]).astype(BF16) for h in range(halves)], axis=0
        )

    def put_sums(target, n, value):
        wide = value.shape[1]
        cells = value.reshape(halves, RUN, SUB, wide)
        sub = iota((HALF, SUB, wide), 1)
        target[n, :, HALF : HALF + RUN] = cells
        before = [pltpu.roll(cells[h, RUN - HALF :], 1, 1) for h in range(halves)]
        after = [pltpu.roll(cells[h, :HALF], SUB - 1, 1) for h in range(halves)]
        zero = jnp.zeros((HALF, SUB, wide), F32)
        for h in range(halves):
            target[n, h, :HALF] = jnp.where(sub == 0, before[h - 1] if h else zero, before[h])
            target[n, h, HALF + RUN :] = jnp.where(
                sub == SUB - 1, after[h + 1] if h + 1 < halves else zero, after[h]
            )

    def row_sums(source, n, h, first, size, lanes):
        v = source[n, h, first : first + size + 6, :, lanes]
        two = v[: size + 5] + v[1 : size + 6]
        four = two[:size] + two[2 : size + 2]
        return (four + two[4 : size + 4]) + v[6 : size + 6]

    stage2(0)
    stage2(REF)
    stage2(1)
    if views > 2:
        stage2(2)
    stage3(0)
    for k in range(zviews, views):
        pass_on(k)
    finish(REF)

    r = permute(ref_all[...].reshape(rows, TW))
    rb[...] = r
    rf = r.astype(F32)
    pack(rf, 0, EDGE_SLOTS)
    rr_hi, rr_lo = split2(rf * rf)
    put_sums(sums_odd, 0, mm(r, band[...]))
    put_sums(sums_odd, 1, mm(rr_hi, band[...]) + mm(rr_lo, band[...]))
    for h in range(halves):
        sr = row_sums(sums_odd, 0, h, 0, RUN, slice(0, TW))
        srr = row_sums(sums_odd, 1, h, 0, RUN, slice(0, TW))
        mean = sr * (1.0 / COUNT)
        rn[h] = mean
        inv[h] = lax.rsqrt(jnp.maximum(srr - sr * mean, 0.0) + STABILIZER)

    STEP = 16

    def bring(v):
        finish(v)
        warp_copy(v).wait()

    def pick(v):
        for b in range(3):
            picked[b] = permute(srcs[v, b].reshape(rows, TW))

    def resample(v, p):
        blocks = [picked[off_ref[p, s, 0, v] + 1] for s in range(4)]
        w = mm(jnp.concatenate(blocks, axis=1), warp[v, p].reshape(4 * TW, TW))
        wb[p] = w.astype(BF16)
        i = v * planes + p
        pack(w, i // EDGE_SLOTS, i % EDGE_SLOTS)

    buffers = (sums_even, sums_odd)

    def box_columns(p):
        target = buffers[p % 2]
        w = wb[p]
        put_sums(target, 0, mm(w, band[...]))
        put_sums(target, 1, mm(w * w, band[...]))
        put_sums(target, 2, mm(w * rb[...], band[...]))

    def correlate(p):
        source = buffers[p % 2]
        for h in range(halves):
            for first in range(0, RUN, STEP):
                for lanes in (slice(0, 128), slice(128, 256)):
                    sw, sww, srw = [row_sums(source, n, h, first, STEP, lanes) for n in range(3)]
                    here = slice(first, first + STEP)
                    covar = srw - rn[h, here, :, lanes] * sw
                    var = jnp.maximum(sww - sw * (sw * (1.0 / COUNT)), 0.0) + STABILIZER
                    acc[p, h, here, :, lanes] += covar * lax.rsqrt(var)

    def view_step(v, carry):
        pl.when(v + 3 < views)(lambda: stage2(v + 3))
        bring(v)
        pick(v)
        for p in range(planes):
            if p == planes // 2:
                stage3(v + 1)
            resample(v, p)
            box_columns((p - 1) % planes)
            correlate((p - 2) % planes)
        return carry

    last = views - 1
    lax.fori_loop(0, last, view_step, 0)
    bring(last)
    pick(last)
    for p in range(planes):
        resample(last, p)
        if p == 0:
            box_columns(planes - 1)
        if p < 2:
            correlate(planes - 2 + p)
    own = jnp.concatenate([slab[n].astype(BF16) for n in range(slabs)], axis=1)
    for g in range(4):
        cells16[g] = mm(own, select[:, 128 * g : 128 * (g + 1)]).astype(BF16)
    for side in (0, 1):
        when_sends(side, lambda side=side: halo_copy(side).start())
    for p in range(planes):
        box_columns(p)
        if p:
            correlate(p - 1)
    correlate(planes - 1)

    def edge_terms(cells, taps):
        refs = [mm(cell, edge_q[...]).astype(BF16) for cell in cells]
        w, rw = jnp.concatenate(cells, axis=1), jnp.concatenate(refs, axis=1)
        wf, rf = w.astype(F32), rw.astype(F32)

        def summed(value):
            hi, lo = split2(value)
            return mm(hi, taps) + mm(lo, taps)

        return [mm(w, taps), summed(wf * wf), summed(rf * wf), mm(rw, taps), summed(rf * rf)]

    for side in (0, 1):
        taps = edge_t[128:] if side == 0 else edge_t[:256]
        for n, term in enumerate(edge_terms([cells16[2 * side], cells16[2 * side + 1]], taps)):
            eparts[side, n] = term

    def in_order(value):
        hi, lo = split2(value * (1.0 / views))
        return 1.0 - (mm(unperm[...], hi) + mm(unperm[...], lo))

    for h in range(halves):
        for p in range(planes):
            cost = in_order((acc[p, h] * inv[h]).reshape(PART, TW))
            vol[p, PART * h : PART * (h + 1)] = cost
            cost4 = cost.reshape(per, 2, rows // nq, TW)
            spot = slice(per * h, per * (h + 1))
            low[spot] = cost4 if p == 0 else jnp.minimum(low[spot], cost4)

    def swap(h, cc):
        return remote(
            low.at[pl.ds(per * h, per), pl.ds(cc, 1)],
            got1.at[pl.ds(per * h, per)],
            p_send.at[h],
            p_recv.at[h],
            (t, sib),
        )

    def min_copy(xx, way):
        return remote(red.at[xx], got2.at[way - 1], m_send.at[way], m_recv.at[way], (t, 2 * xx + c))

    for h in range(halves):
        swap(h, 1 - c).start()

    for side in (0, 1):
        when_arrives(side, lambda side=side: halo_copy(side).wait_recv())
    for h in range(halves):
        swap(h, 1 - c).wait_recv()
    red[...] = jnp.minimum(low[:, pl.ds(c, 1)], got1[...])
    for d in range(1, nx):
        min_copy(at_x(d), d).start()

    edges = []
    for side in (0, 1):
        taps = edge_t[:128] if side == 0 else edge_t[256:]
        for n, term in enumerate(edge_terms([halo[side]], taps)):
            put_sums(esums.at[side], n, eparts[side, n] + term)
        out = []
        for h in range(halves):
            sw, sww, srw, sr, srr = [row_sums(esums.at[side], n, h, 0, RUN, slice(0, 128)) for n in range(5)]
            covar = srw - sr * (sw * (1.0 / COUNT))
            var = jnp.maximum(sww - sw * (sw * (1.0 / COUNT)), 0.0) + STABILIZER
            var_r = jnp.maximum(srr - sr * (sr * (1.0 / COUNT)), 0.0) + STABILIZER
            ncc = covar * (lax.rsqrt(var) * lax.rsqrt(var_r))
            total = ncc
            for v in range(1, views):
                total = total + pltpu.roll(ncc, 128 - 3 * planes * v, 2)
            out.append(in_order(total.reshape(PART, 128)))
        edges.append(out)

    lane2 = iota((PART, 128), 1)
    chip = rows // nx
    for h in range(halves):
        here = slice(PART * h, PART * (h + 1))
        both = []
        for side in (0, 1):
            least = None
            for p in range(planes):
                turned = pltpu.roll(edges[side][h], 125 - 3 * p if side else (128 - 3 * p) % 128, 1)
                least = turned if least is None else jnp.minimum(least, turned)
            both.append(least)
        sides = pltpu.roll(jnp.where(lane2 < 64, both[0], both[1]), 3, 1)
        flat = sides.T
        for n in range(per):
            emin[per * h + n] = flat[:SUB, chip * n : chip * (n + 1)]

    def side_copy(dx, dc):
        n = 2 * dx + dc - 1
        return remote(
            emin.at[at_x(dx)],
            egot.at[n],
            e_send.at[n],
            e_recv.at[n],
            (t, 2 * at_x(dx) + (1 - c if dc else c)),
        )

    others = [(dx, dc) for dx in range(nx) for dc in (0, 1) if dx or dc]
    for dx, dc in others:
        side_copy(dx, dc).start()

    for h in range(halves):
        here = slice(PART * h, PART * (h + 1))
        for side in (0, 1):
            lanes = slice(128 * side, 128 * (side + 1))
            inside = (lane2 >= 125) if side else (lane2 < 3)
            for p in range(planes):
                turned = pltpu.roll(edges[side][h], 125 - 3 * p if side else (128 - 3 * p) % 128, 1)
                vol[p, here, lanes] = jnp.where(inside, turned, vol[p, here, lanes])

    for k in [REF, *range(views)]:
        drain(k)
    for side in (0, 1):
        when_sends(side, lambda side=side: halo_copy(side).wait_send())
    for h in range(halves):
        swap(h, 1 - c).wait_send()

    for d in range(1, nx):
        min_copy(at_x(d), d).wait_recv()
    best = red[x, 0]
    for d in range(1, nx):
        best = jnp.minimum(best, got2[d - 1, 0])
    least = emin[x]
    for dx, dc in others:
        side_copy(dx, dc).wait_recv()
    for dx, dc in others:
        least = jnp.minimum(least, egot[2 * dx + dc - 1])
    part = rows // nq
    etall[...] = jnp.concatenate([least, jnp.zeros((128 - SUB, chip), F32)], axis=0).T
    sides = etall[pl.ds(pl.multiple_of(c * part, part), part)]
    lane1 = iota((part, 128), 1)
    best_ref[:, :128] = jnp.where(lane1 < 3, pltpu.roll(sides, 125, 1), best[:, :128])
    best_ref[:, 128:] = jnp.where(lane1 >= 125, pltpu.roll(sides, 125, 1), best[:, 128:])

    for d in range(1, nx):
        min_copy(at_x(d), d).wait_send()
    for dx, dc in others:
        side_copy(dx, dc).wait_send()


def solution(mesh):
    tiles, nq = mesh.shape["tile"], mesh.shape["plane"]
    nx = nq // 2

    def local(reference_image, source_images, warps, offsets):
        views, planes = warps.shape[0], warps.shape[1]
        part = reference_image.shape[0]
        rows = nq * part
        halves = rows // PART
        slabs = -(-views * planes // EDGE_SLOTS)
        vmem = pltpu.VMEM
        dma = pltpu.SemaphoreType.DMA
        scratch = [
            vmem((views, 3, nx, 2, part, TW), BF16),
            vmem((nx, 2, part, TW), BF16),
            vmem((views, planes, 4, TW, TW), BF16),
            vmem((3, rows, TW), BF16),
            vmem((planes, rows, TW), BF16),
            vmem((rows, TW), BF16),
            vmem((3, halves, RUN + 2 * HALF, SUB, TW), F32),
            vmem((3, halves, RUN + 2 * HALF, SUB, TW), F32),
            vmem((planes, halves, RUN, SUB, TW), F32),
            vmem((halves, RUN, SUB, TW), F32),
            vmem((halves, RUN, SUB, TW), F32),
            vmem((slabs, rows, 128), F32),
            vmem((4, rows, 128), BF16),
            vmem((2, rows, 128), BF16),
            vmem((TW, TW), BF16),
            vmem((TW, TW), BF16),
            vmem((TW, TW), BF16),
            vmem((128 * slabs, 512), BF16),
            vmem((384, 128), BF16),
            vmem((128, 128), BF16),
            vmem((2, 5, halves, RUN + 2 * HALF, SUB, 128), F32),
            vmem((2, 5, rows, 128), F32),
            vmem((nx, 2, part, TW), F32),
            vmem((nx, 1, part, TW), F32),
            vmem((nx, 1, part, TW), F32),
            vmem((nx - 1, 1, part, TW), F32),
            vmem((nx, SUB, 2 * part), F32),
            vmem((nq - 1, SUB, 2 * part), F32),
            vmem((2 * part, 128), F32),
            dma((views + 1, nx - 1)),
            dma((views + 1, nx - 1)),
            dma((views + 1,)),
            dma((views, 2)),
            dma((views, 2)),
            dma((views // 6, 2, nx - 1)),
            dma((views // 6, 2, nx - 1)),
            dma((views + 1, 3)),
            dma((views + 1, 3)),
            dma((views,)),
            dma((2,)),
            dma((2,)),
            dma((halves,)),
            dma((halves,)),
            dma((nx,)),
            dma((nx,)),
            dma((nq - 1,)),
            dma((nq - 1,)),
        ]
        far = pl.BlockSpec(memory_space=pltpu.HBM)
        near = pl.BlockSpec(memory_space=pltpu.VMEM)
        return pl.pallas_call(
            functools.partial(body, views, planes, tiles, nq),
            out_shape=(pltpu.VMEM((planes, rows, TW), F32), pltpu.VMEM((part, TW), F32)),
            in_specs=[far, far, far, pl.BlockSpec(memory_space=pltpu.SMEM)],
            out_specs=(near, near),
            scratch_shapes=scratch,
            compiler_params=pltpu.CompilerParams(
                collective_id=0, has_side_effects=True, vmem_limit_bytes=63300 * 1024
            ),
        )(reference_image, source_images, warps, offsets.transpose(1, 2, 3, 0))

    return jax.shard_map(
        local,
        mesh=mesh,
        in_specs=(
            P("plane", "tile"),
            P(None, "plane", "tile"),
            P(None, "plane", None, None, "tile"),
            P(None, "plane", None, "tile"),
        ),
        out_specs=(P("plane", None, "tile"), P("plane", "tile")),
        check_vma=False,
    )
```
